32 devices in a mesh: atoms: 8 (over z, core), loops: 4 (over y, x).
Axes of the slice: x: 2, y: 2, z: 4, core: 2. Of those that a mesh axis runs over, the one named last changes fastest.
Arguments:
- atom_site: int32 [32768], P('atoms'), may hold values from 0 to 65535, as said below
- loop_cells: int32 [3, 1024], P(None, 'loops'), may hold values from -200 to 199
- loop_burgers: int32 [1024], P('loops'), may hold values from 0 to 3
- loop_habit: int32 [1024], P('loops'), may hold values from 0 to 5
- loop_radius: float32 [1024], P('loops'), may hold values from 10 to 40
Outputs:
- log_intensity: float32 [64, 128, 128], P('loops', 'atoms')
The draws below stay inside these ranges and needn't reach their ends.
Inputs may be any that keep to these rules, and one draw needn't show every extreme that they name: `atom_site`: site numbers are distinct; the first and the last site of the window are always occupied.
All inputs are finite; a program needn't handle non-finite values.
Results may differ from the reference program's by a relative error of at most 0.0003.
Values sent between devices are 32-bit elements; how exact they have to be, the bound alone decides.
A program may use at most 128 MiB of HBM per device.

```python
import math
import jax
import jax.numpy as jnp
import numpy as np
from jax import lax

WIN_X = 32
WIN_Y = 32
LOOP_REACH = 200
QX = 128
QY = 128
QZ = 64
ATOMS = 32768
LOOPS = 1024


def draw_atom_site(key, part):
    inner = jax.random.permutation(key, 2 * ATOMS - 2)[:ATOMS - 2].astype(jnp.int32) + 1
    first = jnp.zeros((1,), jnp.int32)
    last = jnp.full((1,), 2 * ATOMS - 1, jnp.int32)
    return jnp.concatenate([first, inner, last]).astype(jnp.int32)


def plant(entries, own_key, smallest, high):
    spot = [jax.random.randint(jax.random.fold_in(own_key, axis), (), 0, length) for axis, length in enumerate(entries.shape)]
    widest = entries.shape.index(max(entries.shape))
    beside = spot[:widest] + [(spot[widest] + 1) % entries.shape[widest]] + spot[widest + 1:]
    return entries.at[tuple(spot)].set(smallest).at[tuple(beside)].set(high)


def steps_of(stream_key, shape, shards, smallest, high):
    factor_of = 1.0
    for dim, parts in shards:
        steps = jax.random.uniform(jax.random.fold_in(jax.random.fold_in(stream_key, 6), dim), (parts,), jnp.float32, smallest / len(shards), high / len(shards))
        factor_of = factor_of * jnp.repeat(jnp.exp(steps), shape[dim] // parts).reshape((-1,) + (1,) * (len(shape) - 1 - dim))
    return factor_of


def setup_inputs(seed: int = 0) -> dict:
    arg_keys = jax.random.split(jax.random.key(seed), 6)
    return {
        "atom_site": draw_atom_site(jax.random.fold_in(arg_keys[5], 71), 0),
        "loop_cells": plant(jax.random.randint(arg_keys[1], (3, LOOPS), 0 - LOOP_REACH, LOOP_REACH), jax.random.fold_in(arg_keys[1], 1), 0 - LOOP_REACH, LOOP_REACH - 1).astype(jnp.int32),
        "loop_burgers": plant(jax.random.randint(arg_keys[2], (LOOPS,), 0, 4), jax.random.fold_in(arg_keys[2], 1), 0, 3).astype(jnp.int32),
        "loop_habit": plant(jax.random.randint(arg_keys[3], (LOOPS,), 0, 6), jax.random.fold_in(arg_keys[3], 1), 0, 5).astype(jnp.int32),
        "loop_radius": jnp.clip(jnp.exp(math.log(40.0) - 1.3862944 * jax.random.uniform(arg_keys[4], (LOOPS,), jnp.float32) ** steps_of(arg_keys[4], (LOOPS,), ((0, 4),), -0.2, 0.2)), 10.0, 40.0),
    }


LATTICE = 2.8665
POISSON = 0.29
TWO_PI = 2.0 * math.pi
BURGERS_TABLE = np.array([[1.0, 1.0, 1.0], [-1.0, 1.0, 1.0], [1.0, -1.0, 1.0], [1.0, 1.0, -1.0]]) * (0.5 * LATTICE)
NORMAL_TABLE = np.array([[1.0, 1.0, 0.0], [1.0, -1.0, 0.0], [1.0, 0.0, 1.0], [1.0, 0.0, -1.0], [0.0, 1.0, 1.0], [0.0, 1.0, -1.0]]) * 0.70710678

def lookup(index, table):
    columns = []
    for column in range(3):
        total = jnp.zeros(index.shape, jnp.float32)
        for entry in range(table.shape[0]):
            total = total + jnp.where(index == entry, jnp.float32(table[entry, column]), jnp.float32(0.0))
        columns.append(total)
    return jnp.stack(columns)

def site_anchor(site):
    basis = site % 2
    cell = site // 2
    first = cell % WIN_X
    second = cell // WIN_X % WIN_Y
    third = cell // (WIN_X * WIN_Y)
    cells = jnp.stack([first, second, third]).astype(jnp.float32)
    return LATTICE * (cells + 0.5 * basis.astype(jnp.float32)[None, :])

def loop_centre(cells):
    return LATTICE * (cells.astype(jnp.float32) + 0.25)

def loop_field(anchor, centre, burgers, normal, radius):
    offset = anchor[:, None, :] - centre[:, :, None]
    radius_sq = (radius * radius)[:, None]
    distance_sq = lax.optimization_barrier(jnp.sum(offset * offset, axis=0)) + radius_sq
    unit_dir = offset * lax.rsqrt(distance_sq)[None]
    along_b = lax.optimization_barrier(jnp.sum(burgers[:, :, None] * unit_dir, axis=0))
    along_n = lax.optimization_barrier(jnp.sum(normal[:, :, None] * unit_dir, axis=0))
    burgers_normal = lax.optimization_barrier(jnp.sum(burgers * normal, axis=0))[:, None]
    strength = radius_sq / (8.0 * (1.0 - POISSON) * distance_sq)
    field = (1.0 - 2.0 * POISSON) * (burgers[:, :, None] * along_n[None] + normal[:, :, None] * along_b[None])
    field = field - burgers_normal[None] * unit_dir + 3.0 * unit_dir * (along_b * along_n)[None]
    return lax.optimization_barrier(jnp.sum(strength[None] * field, axis=1))

def waves(first, count, total, centre):
    steps = first + jnp.arange(count, dtype=jnp.float32)
    return TWO_PI / LATTICE * (centre + (steps - total * 0.5 + 0.5) / QX)

def factor_block(xcosines, xsines, zcosines, zsines, ytable):
    ywidth = ytable.shape[1] // 2
    left_real = zcosines[None, :, :] * xcosines[:, None, :] - zsines[None, :, :] * xsines[:, None, :]
    left_imag = zcosines[None, :, :] * xsines[:, None, :] + zsines[None, :, :] * xcosines[:, None, :]
    left_pair = jnp.stack([left_real, left_imag], axis=2)
    product = jnp.einsum('xzca,ad->xzcd', left_pair, ytable, precision=lax.Precision.HIGHEST, preferred_element_type=jnp.float32)
    real_part = product[:, :, 0, :ywidth] - product[:, :, 1, ywidth:]
    imag_part = product[:, :, 0, ywidth:] + product[:, :, 1, :ywidth]
    return jnp.stack([real_part, imag_part], axis=1)

def reference(atom_site, loop_cells, loop_burgers, loop_habit, loop_radius):
    anchor = site_anchor(atom_site)
    centre = loop_centre(loop_cells)
    burgers = lookup(loop_burgers, BURGERS_TABLE)
    normal = lookup(loop_habit, NORMAL_TABLE)
    loop_total = centre.shape[1]
    block_size = math.gcd(loop_total, 128)

    def add_block(number, running):
        begin = (number * block_size).astype(jnp.int32)
        return running + loop_field(anchor, lax.dynamic_slice_in_dim(centre, begin, block_size, 1), lax.dynamic_slice_in_dim(burgers, begin, block_size, 1), lax.dynamic_slice_in_dim(normal, begin, block_size, 1), lax.dynamic_slice_in_dim(loop_radius, begin, block_size, 0))
    displacement = lax.fori_loop(0, loop_total // block_size, add_block, jnp.zeros(anchor.shape, jnp.float32))
    position = anchor + displacement
    atom_total = position.shape[1]
    xwaves = waves(jnp.float32(0.0), QX, QX, 1.0)
    ywaves = waves(jnp.float32(0.0), QY, QY, 1.0)
    zwaves = waves(jnp.float32(0.0), QZ, QZ, 0.0)
    xangle = xwaves[:, None] * position[0][None, :]
    yangle = position[1][:, None] * ywaves[None, :]
    zangle = zwaves[:, None] * position[2][None, :]
    xcosines, xsines = (jnp.cos(xangle), jnp.sin(xangle))
    zcosines, zsines = (jnp.cos(zangle), jnp.sin(zangle))
    ytable = jnp.concatenate([jnp.cos(yangle), jnp.sin(yangle)], axis=1)

    def one_plane(plane):
        zc = lax.dynamic_slice_in_dim(zcosines, plane, 1, 0)
        zs = lax.dynamic_slice_in_dim(zsines, plane, 1, 0)
        return factor_block(xcosines, xsines, zc, zs, ytable)[:, :, 0, :]
    amplitude = lax.map(one_plane, jnp.arange(QZ, dtype=jnp.int32))
    power = amplitude[:, :, 0, :] ** 2 + amplitude[:, :, 1, :] ** 2
    return jnp.log1p(power / atom_total)
```

```python
import functools
import math

import jax
import jax.numpy as jnp
import numpy as np
from jax import lax
from jax.experimental import pallas as pl
from jax.experimental.pallas import tpu as pltpu
from jax.sharding import PartitionSpec as P

WIN_X = 32
WIN_Y = 32
QX = 128
QY = 128
QZ = 64
LANES = 128

LATTICE = 2.8665
POISSON = 0.29
MIX = 1.0 - 2.0 * POISSON
BURGERS_TABLE = np.array(
    [[1.0, 1.0, 1.0], [-1.0, 1.0, 1.0], [1.0, -1.0, 1.0], [1.0, 1.0, -1.0]]
) * (0.5 * LATTICE)
NORMAL_TABLE = (
    np.array(
        [
            [1.0, 1.0, 0.0],
            [1.0, -1.0, 0.0],
            [1.0, 0.0, 1.0],
            [1.0, 0.0, -1.0],
            [0.0, 1.0, 1.0],
            [0.0, 1.0, -1.0],
        ]
    )
    * 0.70710678
)


def fit(function, degree):
    nodes = 0.125 * (1.0 + np.cos(np.pi * (np.arange(64) + 0.5) / 64))
    series = np.polynomial.Chebyshev.fit(nodes, function(np.sqrt(nodes)), degree, domain=[0.0, 0.25])
    return [float(c) for c in series.convert(kind=np.polynomial.Polynomial).coef]


COSINE = fit(lambda r: np.cos(2.0 * np.pi * r), 6)
SINE = fit(lambda r: np.sin(2.0 * np.pi * r) / r, 6)


def horner(coefs, u):
    total = jnp.float32(coefs[-1])
    for c in reversed(coefs[:-1]):
        total = total * u + jnp.float32(c)
    return total


def cos_turns(t):
    r = t - jnp.round(t)
    return horner(COSINE, r * r)


def cos_sin_turns(t):
    r = t - jnp.round(t)
    u = r * r
    return horner(COSINE, u), r * horner(SINE, u)


def lookup(index, table, column):
    total = jnp.zeros(index.shape, jnp.float32)
    for entry in range(table.shape[0]):
        total = jnp.where(index == entry, jnp.float32(table[entry, column]), total)
    return total


def field_kernel(
    group_count, site_ref, cells_ref, burgers_ref, habit_ref, radius_ref, out_ref, params_ref, anchor_ref
):
    loops = cells_ref.shape[1]
    chunks = site_ref.shape[0]
    burgers = [lookup(burgers_ref[...], BURGERS_TABLE, c) for c in range(3)]
    normal = [lookup(habit_ref[...], NORMAL_TABLE, c) for c in range(3)]
    centre = [LATTICE * (cells_ref[c : c + 1, :].astype(jnp.float32) + 0.25) for c in range(3)]
    radius_sq = radius_ref[...] * radius_ref[...]
    overlap = burgers[0] * normal[0] + burgers[1] * normal[1] + burgers[2] * normal[2]
    ratio = 3.0 / MIX
    rows = (
        centre
        + [radius_sq]
        + burgers
        + [ratio * n for n in normal]
        + [(1.0 / ratio) * b for b in burgers]
        + normal
        + [(MIX / (8.0 * (1.0 - POISSON))) * radius_sq, (1.0 / MIX) * overlap]
    )
    count = len(rows)
    rows = rows + [jnp.zeros((1, loops), jnp.float32)] * (-count % 8)
    columns = jnp.concatenate(rows, axis=0).T
    for number in range(count):
        params_ref[number] = jnp.broadcast_to(columns[:, number : number + 1], (loops, LANES))

    site = site_ref[...]
    basis = 0.5 * (site & 1).astype(jnp.float32)
    cell = lax.shift_right_logical(site, 1)
    first = lax.rem(cell, WIN_X)
    second = lax.rem(lax.div(cell, WIN_X), WIN_Y)
    third = lax.div(cell, WIN_X * WIN_Y)
    for axis, index in enumerate((first, second, third)):
        anchor_ref[axis] = LATTICE * (index.astype(jnp.float32) + basis)

    width = 2

    def chunk_step(step, _):
        anchors = [
            [
                jnp.broadcast_to(anchor_ref[axis, pl.ds(step * width + w, 1), :], (8, LANES))
                for axis in range(3)
            ]
            for w in range(width)
        ]

        def loop_step(group, sums):
            at = pl.ds(pl.multiple_of(group * 8, 8), 8)
            p = [params_ref[number, at, :] for number in range(count)]
            new = []
            for w in range(width):
                d = [anchors[w][c] - p[c] for c in range(3)]
                s = d[0] * d[0] + d[1] * d[1] + d[2] * d[2] + p[3]
                root = lax.rsqrt(s)
                inv = root * root
                scale = inv * root * p[16]
                along_b = p[4] * d[0] + p[5] * d[1] + p[6] * d[2]
                along_n = p[7] * d[0] + p[8] * d[1] + p[9] * d[2]
                weight_b = scale * along_n
                weight_n = scale * along_b
                weight_d = scale * (along_b * along_n * inv - p[17])
                for c in range(3):
                    new.append(
                        sums[3 * w + c] + (p[10 + c] * weight_b + p[13 + c] * weight_n + d[c] * weight_d)
                    )
            return tuple(new)

        zero = jnp.zeros((8, LANES), jnp.float32)
        sums = lax.fori_loop(0, loops // 8, loop_step, (zero,) * (3 * width), unroll=2)
        for w in range(width):
            for c in range(3):
                total = jnp.sum(sums[3 * w + c], axis=0, keepdims=True)
                out_ref[c, pl.ds(step * width + w, 1), :] = (
                    total + (1.0 / group_count) * anchor_ref[c, pl.ds(step * width + w, 1), :]
                )
        return 0

    lax.fori_loop(0, chunks // width, chunk_step, 0)


def exchange_kernel(na, nl, part_ref, out_ref, landed, send_a, recv_a, send_b, recv_b, send_c, recv_c):
    me_a = lax.axis_index("atoms")
    me_l = lax.axis_index("loops")
    mesh_ids = pl.DeviceIdType.MESH
    peers_a = [lax.rem(me_a + o, na) for o in range(1, na)]
    peers_l = [lax.rem(me_l + o, nl) for o in range(1, nl)]
    barrier = pltpu.get_barrier_semaphore()
    for peer in peers_a:
        pl.semaphore_signal(barrier, inc=1, device_id=(peer, me_l), device_id_type=mesh_ids)
    for peer in peers_l:
        pl.semaphore_signal(barrier, inc=1, device_id=(me_a, peer), device_id_type=mesh_ids)
    pl.semaphore_wait(barrier, na + nl - 2)

    def send(src, dst, send_sem, recv_sem, peer):
        copy = pltpu.make_async_remote_copy(
            src_ref=src,
            dst_ref=dst,
            send_sem=send_sem,
            recv_sem=recv_sem,
            device_id=peer,
            device_id_type=mesh_ids,
        )
        copy.start()
        return copy

    first = [
        send(part_ref.at[peer], landed.at[o], send_a.at[o], recv_a.at[o], (me_a, peer))
        for o, peer in enumerate(peers_l)
    ]
    total = part_ref[me_l]
    for o, copy in enumerate(first):
        copy.wait_recv()
        total = total + landed[o]
    out_ref[0, 0] = total
    second = [
        send(out_ref.at[0, 0], out_ref.at[0, o + 1], send_b.at[o], recv_b.at[o], (peer, me_l))
        for o, peer in enumerate(peers_a)
    ]
    for copy in second:
        copy.wait_recv()
    third = [
        send(out_ref.at[0], out_ref.at[o + 1], send_c.at[o], recv_c.at[o], (me_a, peer))
        for o, peer in enumerate(peers_l)
    ]
    for copy in third:
        copy.wait_recv()
    for copy in first + second + third:
        copy.wait_send()


def split(value):
    high = value.astype(jnp.bfloat16)
    low = (value - high.astype(jnp.float32)).astype(jnp.bfloat16)
    return high, low


def amplitude_kernel(atom_total, zrows, xrows, pos_ref, out_ref, acc_ref):
    slots, _, rows, _ = pos_ref.shape
    zhalf, xhalf, yhalf = zrows // 2, xrows // 2, QY // 2
    inverse = 1.0 / LATTICE
    step = inverse / QX
    xmid = 1.0 + (lax.axis_index("atoms") * xrows + xhalf - QX // 2).astype(jnp.float32) / QX
    zmid = (lax.axis_index("loops") * zrows + zhalf - QZ // 2).astype(jnp.float32) / QX
    wide = LANES

    def sub_iota(count):
        return lax.broadcasted_iota(jnp.int32, (count, wide), 0)

    def half_factors(half):
        number = sub_iota(2 * half)
        is_sine = number >= half
        index = jnp.where(is_sine, number - half, number).astype(jnp.float32)
        return (index + 0.5) * step, jnp.where(is_sine, 0.25, 0.0).astype(jnp.float32)

    zfactor, zshift = half_factors(zhalf)
    xfactor, xshift = half_factors(xhalf)
    fine = (sub_iota(8).astype(jnp.float32) - 3.5) * step
    blocks = yhalf // 16
    coarse_number = sub_iota(8)
    coarse = jnp.where(
        coarse_number < blocks, 4.0 + 8.0 * coarse_number.astype(jnp.float32), 0.5 * yhalf
    ) * step

    def tables(x, y, z):
        ztab = cos_turns(z * zfactor - zshift)
        xtab = cos_turns(x * xfactor - xshift)
        base = (x * xmid + z * zmid + y) * inverse
        base = base - jnp.round(base)
        dr, di = cos_sin_turns(base + y * fine)
        cc, cs = cos_sin_turns(y * coarse)
        left = jnp.concatenate([xtab[n : n + 1, :] * ztab for n in range(2 * xhalf)], axis=0)
        real = [None] * (2 * blocks)
        imag = [None] * (2 * blocks)
        for k in range(blocks):
            c, s = cc[k : k + 1, :], cs[k : k + 1, :]
            rc, rs, ic, is_ = dr * c, dr * s, di * c, di * s
            real[blocks + k], imag[blocks + k] = rc - is_, ic + rs
            real[blocks - 1 - k], imag[blocks - 1 - k] = rc + is_, ic - rs
        turned = jnp.concatenate(real + imag, axis=0)
        right = jnp.concatenate(
            [turned * cc[blocks : blocks + 1, :], turned * cs[blocks : blocks + 1, :]], axis=0
        )
        return split(left) + split(right)

    contract = (((1,), (1,)), ((), ()))

    def dot(a, b):
        return lax.dot_general(a, b, contract, preferred_element_type=jnp.float32)

    acc_ref[...] = jnp.zeros_like(acc_ref)
    mrows = left_rows = 4 * zhalf * xhalf
    pair = min(2, rows)

    def slot_step(slot, _):
        total = None
        for row in range(0, rows, pair):
            parts = []
            for r in range(row, row + pair):
                x, y, z = (pos_ref[slot, c, r : r + 1, :] for c in range(3))
                parts.append(tables(x, y, z))
            lh, ll, rh, rl = (jnp.concatenate([p[n] for p in parts], axis=1) for n in range(4))
            both = dot(jnp.concatenate([lh, ll], axis=0), rh)
            here = both[:mrows] + both[mrows:] + dot(lh, rl)
            total = here if total is None else total + here
        acc_ref[...] += total
        return 0

    lax.fori_loop(0, slots, slot_step, 0)

    acc = acc_ref[...]
    cre, cim = acc[:, :yhalf], acc[:, yhalf : 2 * yhalf]
    sre, sim = acc[:, 2 * yhalf : 3 * yhalf], acc[:, 3 * yhalf :]
    re = jnp.concatenate([cre + sim, cre - sim], axis=1)
    im = jnp.concatenate([cim - sre, cim + sre], axis=1)

    def rows_of(value, xt, mx, zt):
        begin = ((xt * xhalf + mx) * 2 + zt) * zhalf
        return value[begin : begin + zhalf]

    for mx in range(xhalf):
        by_z = {}
        for xt in range(2):
            rc, rs = rows_of(re, xt, mx, 0), rows_of(re, xt, mx, 1)
            ic, is_ = rows_of(im, xt, mx, 0), rows_of(im, xt, mx, 1)
            by_z[xt, 1] = (rc - is_, ic + rs)
            by_z[xt, 0] = (rc + is_, ic - rs)
        for zsign in range(2):
            (rc, ic), (rs, is_) = by_z[0, zsign], by_z[1, zsign]
            for xsign, power in (
                (1, (rc - is_) ** 2 + (ic + rs) ** 2),
                (0, (rc + is_) ** 2 + (ic - rs) ** 2),
            ):
                value = jnp.log1p(power / atom_total)
                xi = xhalf + mx if xsign else xhalf - 1 - mx
                for mz in range(zhalf):
                    zi = zhalf + mz if zsign else zhalf - 1 - mz
                    out_ref[zi, xi : xi + 1, :] = value[mz : mz + 1, :]


def body(na, nl, atom_site, loop_cells, loop_burgers, loop_habit, loop_radius):
    atoms = atom_site.shape[0]
    loops = loop_cells.shape[1]
    chunks = atoms // LANES
    rows = chunks // nl
    vmem = pl.BlockSpec(memory_space=pltpu.VMEM)
    partial_field = pl.pallas_call(
        functools.partial(field_kernel, nl),
        out_shape=jax.ShapeDtypeStruct((3, chunks, LANES), jnp.float32),
        in_specs=[vmem] * 5,
        out_specs=vmem,
        scratch_shapes=[
            pltpu.VMEM((18, loops, LANES), jnp.float32),
            pltpu.VMEM((3, chunks, LANES), jnp.float32),
        ],
        compiler_params=pltpu.CompilerParams(vmem_limit_bytes=32 * 2**20),
        name="loop_field",
    )(
        atom_site.reshape(chunks, LANES),
        loop_cells,
        loop_burgers.reshape(1, loops),
        loop_habit.reshape(1, loops),
        loop_radius.reshape(1, loops),
    )
    pieces = jnp.transpose(partial_field.reshape(3, nl, rows, LANES), (1, 0, 2, 3))
    position = pl.pallas_call(
        functools.partial(exchange_kernel, na, nl),
        out_shape=jax.ShapeDtypeStruct((nl, na, 3, rows, LANES), jnp.float32),
        in_specs=[vmem],
        out_specs=vmem,
        scratch_shapes=[pltpu.VMEM((nl - 1, 3, rows, LANES), jnp.float32)]
        + [pltpu.SemaphoreType.DMA((n - 1,)) for n in (nl, nl, na, na, nl, nl)],
        compiler_params=pltpu.CompilerParams(
            collective_id=0, has_side_effects=True, vmem_limit_bytes=32 * 2**20
        ),
        name="exchange_positions",
    )(pieces)
    zrows, xrows = QZ // nl, QX // na
    return pl.pallas_call(
        functools.partial(amplitude_kernel, float(atoms * na), zrows, xrows),
        out_shape=jax.ShapeDtypeStruct((zrows, xrows, QY), jnp.float32),
        in_specs=[vmem],
        out_specs=vmem,
        scratch_shapes=[pltpu.VMEM((zrows * xrows, 2 * QY), jnp.float32)],
        compiler_params=pltpu.CompilerParams(vmem_limit_bytes=48 * 2**20),
        name="amplitude",
    )(position.reshape(nl * na, 3, rows, LANES))


def solution(mesh):
    placed = (P("atoms"), P(None, "loops"), P("loops"), P("loops"), P("loops"))
    return jax.shard_map(
        functools.partial(body, mesh.shape["atoms"], mesh.shape["loops"]),
        mesh=mesh,
        in_specs=placed,
        out_specs=P("loops", "atoms", None),
        check_vma=False,
    )
```

```python
import functools
import math

import jax
import jax.numpy as jnp
import numpy as np
from jax import lax
from jax.experimental import pallas as pl
from jax.experimental.pallas import tpu as pltpu
from jax.sharding import PartitionSpec as P

WIN_X = 32
WIN_Y = 32
QX = 128
QY = 128
QZ = 64
LANES = 128

LATTICE = 2.8665
POISSON = 0.29
MIX = 1.0 - 2.0 * POISSON
BURGERS_TABLE = np.array(
    [[1.0, 1.0, 1.0], [-1.0, 1.0, 1.0], [1.0, -1.0, 1.0], [1.0, 1.0, -1.0]]
) * (0.5 * LATTICE)
NORMAL_TABLE = (
    np.array(
        [
            [1.0, 1.0, 0.0],
            [1.0, -1.0, 0.0],
            [1.0, 0.0, 1.0],
            [1.0, 0.0, -1.0],
            [0.0, 1.0, 1.0],
            [0.0, 1.0, -1.0],
        ]
    )
    * 0.70710678
)


def fit(function, degree):
    nodes = 0.125 * (1.0 + np.cos(np.pi * (np.arange(64) + 0.5) / 64))
    series = np.polynomial.Chebyshev.fit(nodes, function(np.sqrt(nodes)), degree, domain=[0.0, 0.25])
    return [float(c) for c in series.convert(kind=np.polynomial.Polynomial).coef]


COSINE = fit(lambda r: np.cos(2.0 * np.pi * r), 6)
SINE = fit(lambda r: np.sin(2.0 * np.pi * r) / r, 6)


def horner(coefs, u):
    total = jnp.float32(coefs[-1])
    for c in reversed(coefs[:-1]):
        total = total * u + jnp.float32(c)
    return total


def cos_turns(t):
    r = t - jnp.round(t)
    return horner(COSINE, r * r)


def cos_sin_turns(t):
    r = t - jnp.round(t)
    u = r * r
    return horner(COSINE, u), r * horner(SINE, u)


def lookup(index, table, column):
    total = jnp.zeros(index.shape, jnp.float32)
    for entry in range(table.shape[0]):
        total = jnp.where(index == entry, jnp.float32(table[entry, column]), total)
    return total


def field_phase(
    nl, site_ref, cells_ref, burgers_ref, habit_ref, radius_ref, part_ref, params_ref, anchor_ref
):
    loops = cells_ref.shape[1]
    chunks = site_ref.shape[0]
    rows_each = part_ref.shape[2]
    burgers = [lookup(burgers_ref[...], BURGERS_TABLE, c) for c in range(3)]
    normal = [lookup(habit_ref[...], NORMAL_TABLE, c) for c in range(3)]
    centre = [LATTICE * (cells_ref[c : c + 1, :].astype(jnp.float32) + 0.25) for c in range(3)]
    radius_sq = radius_ref[...] * radius_ref[...]
    overlap = burgers[0] * normal[0] + burgers[1] * normal[1] + burgers[2] * normal[2]
    ratio = 3.0 / MIX
    rows = (
        centre
        + [radius_sq]
        + burgers
        + [ratio * n for n in normal]
        + [(1.0 / ratio) * b for b in burgers]
        + normal
        + [(MIX / (8.0 * (1.0 - POISSON))) * radius_sq, (1.0 / MIX) * overlap]
    )
    count = len(rows)
    rows = rows + [jnp.zeros((1, loops), jnp.float32)] * (-count % 8)
    columns = jnp.concatenate(rows, axis=0).T
    for number in range(count):
        params_ref[number] = jnp.broadcast_to(columns[:, number : number + 1], (loops, LANES))

    site = site_ref[...]
    basis = 0.5 * (site & 1).astype(jnp.float32)
    cell = lax.shift_right_logical(site, 1)
    first = lax.rem(cell, WIN_X)
    second = lax.rem(lax.div(cell, WIN_X), WIN_Y)
    third = lax.div(cell, WIN_X * WIN_Y)
    for axis, index in enumerate((first, second, third)):
        anchor_ref[axis] = LATTICE * (index.astype(jnp.float32) + basis)

    width = 4

    def chunk_step(step, _):
        anchors = [
            [
                jnp.broadcast_to(anchor_ref[axis, pl.ds(step * width + w, 1), :], (8, LANES))
                for axis in range(3)
            ]
            for w in range(width)
        ]

        def loop_step(group, sums):
            at = pl.ds(pl.multiple_of(group * 8, 8), 8)
            p = [params_ref[number, at, :] for number in range(count)]
            new = []
            for w in range(width):
                d = [anchors[w][c] - p[c] for c in range(3)]
                s = d[0] * d[0] + d[1] * d[1] + d[2] * d[2] + p[3]
                root = lax.rsqrt(s)
                inv = root * root
                scale = inv * root * p[16]
                along_b = p[4] * d[0] + p[5] * d[1] + p[6] * d[2]
                along_n = p[7] * d[0] + p[8] * d[1] + p[9] * d[2]
                weight_b = scale * along_n
                weight_n = scale * along_b
                weight_d = scale * (along_b * along_n * inv - p[17])
                for c in range(3):
                    new.append(
                        sums[3 * w + c] + (p[10 + c] * weight_b + p[13 + c] * weight_n + d[c] * weight_d)
                    )
            return tuple(new)

        zero = jnp.zeros((8, LANES), jnp.float32)
        sums = lax.fori_loop(0, loops // 8, loop_step, (zero,) * (3 * width), unroll=2)
        for w in range(width):
            chunk = step * width + w
            for c in range(3):
                total = jnp.sum(sums[3 * w + c], axis=0, keepdims=True)
                part_ref[lax.div(chunk, rows_each), c, pl.ds(lax.rem(chunk, rows_each), 1), :] = (
                    total + (1.0 / nl) * anchor_ref[c, pl.ds(chunk, 1), :]
                )
        return 0

    lax.fori_loop(0, chunks // width, chunk_step, 0)


def split(value):
    high = value.astype(jnp.bfloat16)
    low = (value - high.astype(jnp.float32)).astype(jnp.bfloat16)
    return high, low


def whole_kernel(
    na, nl, atom_total,
    site_ref, cells_ref, burgers_ref, habit_ref, radius_ref, out_ref,
    params_ref, anchor_ref, part_ref, landed_ref, pos_ref, acc_ref,
    left0, right0, left1, right1, own_ref, give_ref, take_ref,
    send_a, recv_a, send_b, recv_b, send_c, recv_c, send_d, recv_d,
):
    me_a = lax.axis_index("atoms")
    me_l = lax.axis_index("loops")
    mesh_ids = pl.DeviceIdType.MESH
    chips = na // 2
    core = lax.rem(me_a, 2)
    peers_a = [lax.rem(me_a + 2 * o, na) for o in range(1, chips)]
    peers_l = [lax.rem(me_l + o, nl) for o in range(1, nl)]
    partner = me_a + 1 - 2 * core
    barrier = pltpu.get_barrier_semaphore()
    for peer in peers_a + [partner]:
        pl.semaphore_signal(barrier, inc=1, device_id=(peer, me_l), device_id_type=mesh_ids)
    for peer in peers_l:
        pl.semaphore_signal(barrier, inc=1, device_id=(me_a, peer), device_id_type=mesh_ids)

    field_phase(
        nl, site_ref, cells_ref, burgers_ref, habit_ref, radius_ref, part_ref, params_ref, anchor_ref
    )
    pl.semaphore_wait(barrier, chips + nl - 1)

    def send(src, dst, send_sem, recv_sem, peer):
        copy = pltpu.make_async_remote_copy(
            src_ref=src,
            dst_ref=dst,
            send_sem=send_sem,
            recv_sem=recv_sem,
            device_id=peer,
            device_id_type=mesh_ids,
        )
        copy.start()
        return copy

    first = [
        send(part_ref.at[peer], landed_ref.at[o], send_a.at[o], recv_a.at[o], (me_a, peer))
        for o, peer in enumerate(peers_l)
    ]

    zrows, xhalf, _ = out_ref.shape
    zhalf, yhalf = zrows // 2, QY // 2
    rows = pos_ref.shape[3]
    half = rows // 2
    inverse = 1.0 / LATTICE
    unit = inverse / QX
    pair = lax.div(me_a, 2)
    xmid = 1.0 + (pair * (2 * xhalf) + xhalf - QX // 2).astype(jnp.float32) / QX
    zmid = (me_l * zrows + zhalf - QZ // 2).astype(jnp.float32) / QX

    def sub_iota(count):
        return lax.broadcasted_iota(jnp.int32, (count, LANES), 0)

    znumber = sub_iota(2 * zhalf)
    zsine = znumber >= zhalf
    zfactor = (jnp.where(zsine, znumber - zhalf, znumber).astype(jnp.float32) + 0.5) * unit
    zshift = jnp.where(zsine, 0.25, 0.0).astype(jnp.float32)
    xfactor = (sub_iota(xhalf).astype(jnp.float32) + 0.5) * unit
    fine = (sub_iota(8).astype(jnp.float32) - 3.5) * unit
    blocks = yhalf // 16
    coarse_number = sub_iota(8)
    coarse = jnp.where(
        coarse_number < blocks, 4.0 + 8.0 * coarse_number.astype(jnp.float32), 0.5 * yhalf
    ) * unit

    def tables(x, y, z):
        ztab = cos_turns(z * zfactor - zshift)
        xtab = cos_sin_turns(x * xfactor)
        base = (x * xmid + z * zmid + y) * inverse
        base = base - jnp.round(base)
        dr, di = cos_sin_turns(base + y * fine)
        cc, cs = cos_sin_turns(y * coarse)
        left = jnp.concatenate(
            [xtab[t][n : n + 1, :] * ztab for t in range(2) for n in range(xhalf)], axis=0
        )
        real = [None] * (2 * blocks)
        imag = [None] * (2 * blocks)
        for k in range(blocks):
            c, s = cc[k : k + 1, :], cs[k : k + 1, :]
            rc, rs, ic, is_ = dr * c, dr * s, di * c, di * s
            real[blocks + k], imag[blocks + k] = rc - is_, ic + rs
            real[blocks - 1 - k], imag[blocks - 1 - k] = rc + is_, ic - rs
        turned = jnp.concatenate(real + imag, axis=0)
        right = jnp.concatenate(
            [turned * cc[blocks : blocks + 1, :], turned * cs[blocks : blocks + 1, :]], axis=0
        )
        return split(left), split(right)

    def build(quarter, slot, begin, left_ref, right_ref):
        for r in range(half):
            x, y, z = (pos_ref[quarter, slot, c, begin + r : begin + r + 1, :] for c in range(3))
            left, right = tables(x, y, z)
            lanes = slice(r * LANES, (r + 1) * LANES)
            for n in range(2):
                left_ref[n, :, lanes] = left[n]
                right_ref[n, :, lanes] = right[n]

    def multiply(left_ref, right_ref):
        lh, ll, rh, rl = left_ref[0], left_ref[1], right_ref[0], right_ref[1]
        acc_ref[...] += lax.dot_general(
            jnp.concatenate([lh, ll, lh], axis=1),
            jnp.concatenate([rh, rh, rl], axis=1),
            (((1,), (1,)), ((), ())),
            preferred_element_type=jnp.float32,
        )

    def process(quarter, begin, end):
        def step(slot, _):
            build(quarter, slot, 0, left0, right0)
            multiply(left1, right1)
            build(quarter, slot, half, left1, right1)
            multiply(left0, right0)
            return 0

        lax.fori_loop(begin, end, step, 0)

    acc_ref[...] = jnp.zeros_like(acc_ref)
    left1[...] = jnp.zeros_like(left1)
    right1[...] = jnp.zeros_like(right1)
    total = part_ref[me_l]
    for o, copy in enumerate(first):
        copy.wait_recv()
        total = total + landed_ref[o]
    pos_ref[0, 0] = total
    second = [
        send(pos_ref.at[0, 0], pos_ref.at[0, o + 1], send_b.at[o], recv_b.at[o], (peer, me_l))
        for o, peer in enumerate(peers_a)
    ]
    process(0, 0, 1)
    for copy in second:
        copy.wait_recv()
    third = [
        send(pos_ref.at[0], pos_ref.at[o + 1], send_c.at[o], recv_c.at[o], (me_a, peer))
        for o, peer in enumerate(peers_l)
    ]
    process(0, 1, chips)
    for o, copy in enumerate(third):
        copy.wait_recv()
        process(o + 1, 0, chips)
    multiply(left1, right1)

    mine = (2 * core - 1).astype(jnp.float32)
    width = 2 * zhalf

    def combine(begin):
        block = acc_ref[begin : begin + width, :]
        cre, cim = block[:, :yhalf], block[:, yhalf : 2 * yhalf]
        sre, sim = block[:, 2 * yhalf : 3 * yhalf], block[:, 3 * yhalf :]
        re = jnp.concatenate([cre + sim, cre - sim], axis=1)
        im = jnp.concatenate([cim - sre, cim + sre], axis=1)
        rc, rs, ic, is_ = re[:zhalf], re[zhalf:], im[:zhalf], im[zhalf:]
        return ((rc + is_, ic - rs), (rc - is_, ic + rs))

    pieces = math.gcd(4, xhalf)
    each = xhalf // pieces
    fourth = []
    for piece in range(pieces):
        for mx in range(piece * each, (piece + 1) * each):
            of_cos = combine(mx * width)
            of_sin = combine((xhalf + mx) * width)
            for zsign in range(2):
                rc, ic = of_cos[zsign]
                rs, is_ = of_sin[zsign][0] * mine, of_sin[zsign][1] * mine
                own_ref[mx, zsign, 0], own_ref[mx, zsign, 1] = rc - is_, ic + rs
                give_ref[mx, zsign, 0], give_ref[mx, zsign, 1] = rc + is_, ic - rs
        at = pl.ds(piece * each, each)
        fourth.append(
            send(give_ref.at[at], take_ref.at[at], send_d.at[piece], recv_d.at[piece], (partner, me_l))
        )
    for piece in range(pieces):
        fourth[piece].wait_recv()
        for mx in range(piece * each, (piece + 1) * each):
            place = core * mx + (1 - core) * (xhalf - 1 - mx)
            for zsign in range(2):
                re = own_ref[mx, zsign, 0] + take_ref[mx, zsign, 0]
                im = own_ref[mx, zsign, 1] + take_ref[mx, zsign, 1]
                value = jnp.log1p((re * re + im * im) / atom_total)
                for mz in range(zhalf):
                    zi = zhalf + mz if zsign else zhalf - 1 - mz
                    out_ref[zi, pl.ds(place, 1), :] = value[mz : mz + 1, :]
    for copy in first + second + third + fourth:
        copy.wait_send()


def body(na, nl, atom_site, loop_cells, loop_burgers, loop_habit, loop_radius):
    atoms = atom_site.shape[0]
    loops = loop_cells.shape[1]
    chunks = atoms // LANES
    rows = chunks // nl
    zrows, xrows = QZ // nl, QX // na
    height = 2 * zrows * xrows
    depth = rows // 2 * LANES
    vmem = pl.BlockSpec(memory_space=pltpu.VMEM)
    f32, bf16 = jnp.float32, jnp.bfloat16
    half_block = (xrows, 2, 2, zrows // 2, QY)
    scratch = [
        pltpu.VMEM((18, loops, LANES), f32),
        pltpu.VMEM((3, chunks, LANES), f32),
        pltpu.VMEM((nl, 3, rows, LANES), f32),
        pltpu.VMEM((nl - 1, 3, rows, LANES), f32),
        pltpu.VMEM((nl, na // 2, 3, rows, LANES), f32),
        pltpu.VMEM((height, 2 * QY), f32),
        pltpu.VMEM((2, height, depth), bf16),
        pltpu.VMEM((2, 2 * QY, depth), bf16),
        pltpu.VMEM((2, height, depth), bf16),
        pltpu.VMEM((2, 2 * QY, depth), bf16),
    ] + [pltpu.VMEM(half_block, f32)] * 3
    counts = (nl - 1, nl - 1, na // 2 - 1, na // 2 - 1, nl - 1, nl - 1, 4, 4)
    scratch += [pltpu.SemaphoreType.DMA((n,)) for n in counts]
    return pl.pallas_call(
        functools.partial(whole_kernel, na, nl, float(atoms * na)),
        out_shape=jax.ShapeDtypeStruct((zrows, xrows, QY), f32),
        in_specs=[vmem] * 5,
        out_specs=vmem,
        scratch_shapes=scratch,
        compiler_params=pltpu.CompilerParams(
            collective_id=0, has_side_effects=True, vmem_limit_bytes=48 * 2**20
        ),
        name="diffuse",
    )(
        atom_site.reshape(chunks, LANES),
        loop_cells,
        loop_burgers.reshape(1, loops),
        loop_habit.reshape(1, loops),
        loop_radius.reshape(1, loops),
    )


def solution(mesh):
    placed = (P("atoms"), P(None, "loops"), P("loops"), P("loops"), P("loops"))
    return jax.shard_map(
        functools.partial(body, mesh.shape["atoms"], mesh.shape["loops"]),
        mesh=mesh,
        in_specs=placed,
        out_specs=P("loops", "atoms", None),
        check_vma=False,
    )
```

```python
import functools
import math

import jax
import jax.numpy as jnp
import numpy as np
from jax import lax
from jax.experimental import pallas as pl
from jax.experimental.pallas import tpu as pltpu
from jax.sharding import PartitionSpec as P

WIN_X = 32
WIN_Y = 32
QX = 128
QY = 128
QZ = 64
LANES = 128
SCALE = 128.0
SMALL = jnp.float8_e4m3fn

LATTICE = 2.8665
POISSON = 0.29
MIX = 1.0 - 2.0 * POISSON
BURGERS_TABLE = np.array(
    [[1.0, 1.0, 1.0], [-1.0, 1.0, 1.0], [1.0, -1.0, 1.0], [1.0, 1.0, -1.0]]
) * (0.5 * LATTICE)
NORMAL_TABLE = (
    np.array(
        [
            [1.0, 1.0, 0.0],
            [1.0, -1.0, 0.0],
            [1.0, 0.0, 1.0],
            [1.0, 0.0, -1.0],
            [0.0, 1.0, 1.0],
            [0.0, 1.0, -1.0],
        ]
    )
    * 0.70710678
)


def fit(function, degree):
    nodes = 0.125 * (1.0 + np.cos(np.pi * (np.arange(64) + 0.5) / 64))
    series = np.polynomial.Chebyshev.fit(nodes, function(np.sqrt(nodes)), degree, domain=[0.0, 0.25])
    return [float(c) for c in series.convert(kind=np.polynomial.Polynomial).coef]


COSINE = fit(lambda r: np.cos(2.0 * np.pi * r), 6)
SINE = fit(lambda r: np.sin(2.0 * np.pi * r) / r, 6)


def horner(coefs, u):
    total = jnp.float32(coefs[-1])
    for c in reversed(coefs[:-1]):
        total = total * u + jnp.float32(c)
    return total


def cos_turns(t):
    r = t - jnp.round(t)
    return horner(COSINE, r * r)


def cos_sin_turns(t):
    r = t - jnp.round(t)
    u = r * r
    return horner(COSINE, u), r * horner(SINE, u)


def lookup(index, table, column):
    total = jnp.zeros(index.shape, jnp.float32)
    for entry in range(table.shape[0]):
        total = jnp.where(index == entry, jnp.float32(table[entry, column]), total)
    return total


def field_phase(
    nl, site_ref, cells_ref, burgers_ref, habit_ref, radius_ref, part_ref, params_ref, anchor_ref
):
    loops = cells_ref.shape[1]
    chunks = site_ref.shape[0]
    rows_each = part_ref.shape[2]
    burgers = [lookup(burgers_ref[...], BURGERS_TABLE, c) for c in range(3)]
    normal = [lookup(habit_ref[...], NORMAL_TABLE, c) for c in range(3)]
    centre = [LATTICE * (cells_ref[c : c + 1, :].astype(jnp.float32) + 0.25) for c in range(3)]
    radius_sq = radius_ref[...] * radius_ref[...]
    overlap = burgers[0] * normal[0] + burgers[1] * normal[1] + burgers[2] * normal[2]
    ratio = 3.0 / MIX
    rows = (
        centre
        + [radius_sq]
        + burgers
        + [ratio * n for n in normal]
        + [(1.0 / ratio) * b for b in burgers]
        + normal
        + [(MIX / (8.0 * (1.0 - POISSON))) * radius_sq, (1.0 / MIX) * overlap]
    )
    count = len(rows)
    rows = rows + [jnp.zeros((1, loops), jnp.float32)] * (-count % 8)
    columns = jnp.concatenate(rows, axis=0).T
    for number in range(count):
        params_ref[number] = jnp.broadcast_to(columns[:, number : number + 1], (loops, LANES))

    site = site_ref[...]
    basis = 0.5 * (site & 1).astype(jnp.float32)
    cell = lax.shift_right_logical(site, 1)
    first = lax.rem(cell, WIN_X)
    second = lax.rem(lax.div(cell, WIN_X), WIN_Y)
    third = lax.div(cell, WIN_X * WIN_Y)
    for axis, index in enumerate((first, second, third)):
        anchor_ref[axis] = LATTICE * (index.astype(jnp.float32) + basis)

    width = 4

    def chunk_step(step, _):
        anchors = [
            [
                jnp.broadcast_to(anchor_ref[axis, pl.ds(step * width + w, 1), :], (8, LANES))
                for axis in range(3)
            ]
            for w in range(width)
        ]

        def loop_step(group, sums):
            at = pl.ds(pl.multiple_of(group * 8, 8), 8)
            p = [params_ref[number, at, :] for number in range(count)]
            new = []
            for w in range(width):
                d = [anchors[w][c] - p[c] for c in range(3)]
                s = d[0] * d[0] + d[1] * d[1] + d[2] * d[2] + p[3]
                root = lax.rsqrt(s)
                inv = root * root
                scale = inv * root * p[16]
                along_b = p[4] * d[0] + p[5] * d[1] + p[6] * d[2]
                along_n = p[7] * d[0] + p[8] * d[1] + p[9] * d[2]
                weight_b = scale * along_n
                weight_n = scale * along_b
                weight_d = scale * (along_b * along_n * inv - p[17])
                for c in range(3):
                    new.append(
                        sums[3 * w + c] + (p[10 + c] * weight_b + p[13 + c] * weight_n + d[c] * weight_d)
                    )
            return tuple(new)

        zero = jnp.zeros((8, LANES), jnp.float32)
        sums = lax.fori_loop(0, loops // 8, loop_step, (zero,) * (3 * width), unroll=2)
        for w in range(width):
            chunk = step * width + w
            for c in range(3):
                total = jnp.sum(sums[3 * w + c], axis=0, keepdims=True)
                part_ref[lax.div(chunk, rows_each), c, pl.ds(lax.rem(chunk, rows_each), 1), :] = (
                    total + (1.0 / nl) * anchor_ref[c, pl.ds(chunk, 1), :]
                )
        return 0

    lax.fori_loop(0, chunks // width, chunk_step, 0)


def split(value):
    high = value.astype(jnp.bfloat16)
    low = value - high.astype(jnp.float32)
    return high, value.astype(SMALL), low.astype(SMALL)


def whole_kernel(
    na, nl, atom_total,
    site_ref, cells_ref, burgers_ref, habit_ref, radius_ref, out_ref,
    params_ref, anchor_ref, part_ref, landed_ref, pos_ref, acc_ref,
    tabs0, tabs1, own_ref, give_ref, take_ref,
    send_a, recv_a, send_b, recv_b, send_c, recv_c, send_d, recv_d,
):
    me_a = lax.axis_index("atoms")
    me_l = lax.axis_index("loops")
    mesh_ids = pl.DeviceIdType.MESH
    chips = na // 2
    core = lax.rem(me_a, 2)
    peers_a = [lax.rem(me_a + 2 * o, na) for o in range(1, chips)]
    peers_l = [lax.rem(me_l + o, nl) for o in range(1, nl)]
    partner = me_a + 1 - 2 * core
    barrier = pltpu.get_barrier_semaphore()
    for peer in peers_a + [partner]:
        pl.semaphore_signal(barrier, inc=1, device_id=(peer, me_l), device_id_type=mesh_ids)
    for peer in peers_l:
        pl.semaphore_signal(barrier, inc=1, device_id=(me_a, peer), device_id_type=mesh_ids)

    field_phase(
        nl, site_ref, cells_ref, burgers_ref, habit_ref, radius_ref, part_ref, params_ref, anchor_ref
    )
    pl.semaphore_wait(barrier, chips + nl - 1)

    def send(src, dst, send_sem, recv_sem, peer):
        copy = pltpu.make_async_remote_copy(
            src_ref=src,
            dst_ref=dst,
            send_sem=send_sem,
            recv_sem=recv_sem,
            device_id=peer,
            device_id_type=mesh_ids,
        )
        copy.start()
        return copy

    first = [
        send(part_ref.at[peer], landed_ref.at[o], send_a.at[o], recv_a.at[o], (me_a, peer))
        for o, peer in enumerate(peers_l)
    ]

    zrows, xhalf, _ = out_ref.shape
    zhalf, yhalf = zrows // 2, QY // 2
    rows = pos_ref.shape[3]
    half = rows // 2
    inverse = 1.0 / LATTICE
    unit = inverse / QX
    pair = lax.div(me_a, 2)
    xmid = 1.0 + (pair * (2 * xhalf) + xhalf - QX // 2).astype(jnp.float32) / QX
    zmid = (me_l * zrows + zhalf - QZ // 2).astype(jnp.float32) / QX

    def sub_iota(count):
        return lax.broadcasted_iota(jnp.int32, (count, LANES), 0)

    znumber = sub_iota(2 * zhalf)
    zsine = znumber >= zhalf
    zfactor = (jnp.where(zsine, znumber - zhalf, znumber).astype(jnp.float32) + 0.5) * unit
    zshift = jnp.where(zsine, 0.25, 0.0).astype(jnp.float32)
    xfactor = (sub_iota(xhalf).astype(jnp.float32) + 0.5) * unit
    fine = (sub_iota(8).astype(jnp.float32) - 3.5) * unit
    blocks = yhalf // 16
    coarse_number = sub_iota(8)
    coarse = jnp.where(
        coarse_number < blocks, 4.0 + 8.0 * coarse_number.astype(jnp.float32), 0.5 * yhalf
    ) * unit

    def tables(x, y, z):
        ztab = SCALE * cos_turns(z * zfactor - zshift)
        xtab = cos_sin_turns(x * xfactor)
        base = (x * xmid + z * zmid + y) * inverse
        base = base - jnp.round(base)
        dr, di = cos_sin_turns(base + y * fine)
        dr, di = SCALE * dr, SCALE * di
        cc, cs = cos_sin_turns(y * coarse)
        left = jnp.concatenate(
            [xtab[t][n : n + 1, :] * ztab for t in range(2) for n in range(xhalf)], axis=0
        )
        real = [None] * (2 * blocks)
        imag = [None] * (2 * blocks)
        for k in range(blocks):
            c, s = cc[k : k + 1, :], cs[k : k + 1, :]
            rc, rs, ic, is_ = dr * c, dr * s, di * c, di * s
            real[blocks + k], imag[blocks + k] = rc - is_, ic + rs
            real[blocks - 1 - k], imag[blocks - 1 - k] = rc + is_, ic - rs
        turned = jnp.concatenate(real + imag, axis=0)
        right = jnp.concatenate(
            [turned * cc[blocks : blocks + 1, :], turned * cs[blocks : blocks + 1, :]], axis=0
        )
        return split(left), split(right)

    def build(quarter, slot, begin, tabs):
        for r in range(half):
            x, y, z = (pos_ref[quarter, slot, c, begin + r : begin + r + 1, :] for c in range(3))
            left, right = tables(x, y, z)
            lanes = slice(r * LANES, (r + 1) * LANES)
            for n, value in enumerate(left + right):
                tabs[n][:, lanes] = value

    def dot(a, b):
        return lax.dot_general(
            a, b, (((1,), (1,)), ((), ())), preferred_element_type=jnp.float32
        )

    def multiply(tabs):
        lh, lq, ll, rh, rq, rl = (ref[...] for ref in tabs)
        small = dot(jnp.concatenate([ll, lq], axis=1), jnp.concatenate([rq, rl], axis=1))
        acc_ref[...] += dot(lh, rh) + small

    def process(quarter, begin, end):
        def step(slot, _):
            build(quarter, slot, 0, tabs0)
            multiply(tabs1)
            build(quarter, slot, half, tabs1)
            multiply(tabs0)
            return 0

        lax.fori_loop(begin, end, step, 0)

    acc_ref[...] = jnp.zeros_like(acc_ref)
    for ref in tabs1:
        ref[...] = jnp.zeros_like(ref)
    total = part_ref[me_l]
    for o, copy in enumerate(first):
        copy.wait_recv()
        total = total + landed_ref[o]
    pos_ref[0, 0] = total
    second = [
        send(pos_ref.at[0, 0], pos_ref.at[0, o + 1], send_b.at[o], recv_b.at[o], (peer, me_l))
        for o, peer in enumerate(peers_a)
    ]
    process(0, 0, 1)
    for copy in second:
        copy.wait_recv()
    third = [
        send(pos_ref.at[0], pos_ref.at[o + 1], send_c.at[o], recv_c.at[o], (me_a, peer))
        for o, peer in enumerate(peers_l)
    ]
    process(0, 1, chips)
    for o, copy in enumerate(third):
        copy.wait_recv()
        process(o + 1, 0, chips)
    multiply(tabs1)

    mine = (2 * core - 1).astype(jnp.float32)
    width = 2 * zhalf

    def combine(begin):
        block = acc_ref[begin : begin + width, :]
        cre, cim = block[:, :yhalf], block[:, yhalf : 2 * yhalf]
        sre, sim = block[:, 2 * yhalf : 3 * yhalf], block[:, 3 * yhalf :]
        re = jnp.concatenate([cre + sim, cre - sim], axis=1)
        im = jnp.concatenate([cim - sre, cim + sre], axis=1)
        rc, rs, ic, is_ = re[:zhalf], re[zhalf:], im[:zhalf], im[zhalf:]
        return ((rc + is_, ic - rs), (rc - is_, ic + rs))

    pieces = math.gcd(4, xhalf)
    each = xhalf // pieces
    fourth = []
    for piece in range(pieces):
        for mx in range(piece * each, (piece + 1) * each):
            of_cos = combine(mx * width)
            of_sin = combine((xhalf + mx) * width)
            for zsign in range(2):
                rc, ic = of_cos[zsign]
                rs, is_ = of_sin[zsign][0] * mine, of_sin[zsign][1] * mine
                own_ref[mx, zsign, 0], own_ref[mx, zsign, 1] = rc - is_, ic + rs
                give_ref[mx, zsign, 0], give_ref[mx, zsign, 1] = rc + is_, ic - rs
        at = pl.ds(piece * each, each)
        fourth.append(
            send(give_ref.at[at], take_ref.at[at], send_d.at[piece], recv_d.at[piece], (partner, me_l))
        )
    for piece in range(pieces):
        fourth[piece].wait_recv()
        for mx in range(piece * each, (piece + 1) * each):
            place = core * mx + (1 - core) * (xhalf - 1 - mx)
            for zsign in range(2):
                re = own_ref[mx, zsign, 0] + take_ref[mx, zsign, 0]
                im = own_ref[mx, zsign, 1] + take_ref[mx, zsign, 1]
                value = jnp.log1p((re * re + im * im) / atom_total)
                for mz in range(zhalf):
                    zi = zhalf + mz if zsign else zhalf - 1 - mz
                    out_ref[zi, pl.ds(place, 1), :] = value[mz : mz + 1, :]
    for copy in first + second + third + fourth:
        copy.wait_send()


def body(na, nl, atom_site, loop_cells, loop_burgers, loop_habit, loop_radius):
    atoms = atom_site.shape[0]
    loops = loop_cells.shape[1]
    chunks = atoms // LANES
    rows = chunks // nl
    zrows, xrows = QZ // nl, QX // na
    height = 2 * zrows * xrows
    depth = rows // 2 * LANES
    vmem = pl.BlockSpec(memory_space=pltpu.VMEM)
    f32, bf16 = jnp.float32, jnp.bfloat16
    half_block = (xrows, 2, 2, zrows // 2, QY)
    scratch = [
        pltpu.VMEM((18, loops, LANES), f32),
        pltpu.VMEM((3, chunks, LANES), f32),
        pltpu.VMEM((nl, 3, rows, LANES), f32),
        pltpu.VMEM((nl - 1, 3, rows, LANES), f32),
        pltpu.VMEM((nl, na // 2, 3, rows, LANES), f32),
        pltpu.VMEM((height, 2 * QY), f32),
    ]
    table = tuple(
        pltpu.VMEM((count, depth), kind) for count in (height, 2 * QY) for kind in (bf16, SMALL, SMALL)
    )
    scratch += [table, table]
    scratch += [pltpu.VMEM(half_block, f32)] * 3
    counts = (nl - 1, nl - 1, na // 2 - 1, na // 2 - 1, nl - 1, nl - 1, 4, 4)
    scratch += [pltpu.SemaphoreType.DMA((n,)) for n in counts]
    return pl.pallas_call(
        functools.partial(whole_kernel, na, nl, SCALE**4 * atoms * na),
        out_shape=jax.ShapeDtypeStruct((zrows, xrows, QY), f32),
        in_specs=[vmem] * 5,
        out_specs=vmem,
        scratch_shapes=scratch,
        compiler_params=pltpu.CompilerParams(
            collective_id=0, has_side_effects=True, vmem_limit_bytes=48 * 2**20
        ),
        name="diffuse",
    )(
        atom_site.reshape(chunks, LANES),
        loop_cells,
        loop_burgers.reshape(1, loops),
        loop_habit.reshape(1, loops),
        loop_radius.reshape(1, loops),
    )


def solution(mesh):
    placed = (P("atoms"), P(None, "loops"), P("loops"), P("loops"), P("loops"))
    return jax.shard_map(
        functools.partial(body, mesh.shape["atoms"], mesh.shape["loops"]),
        mesh=mesh,
        in_specs=placed,
        out_specs=P("loops", "atoms", None),
        check_vma=False,
    )
```

```python
import functools
import math

import jax
import jax.numpy as jnp
import numpy as np
from jax import lax
from jax.experimental import pallas as pl
from jax.experimental.pallas import tpu as pltpu
from jax.sharding import PartitionSpec as P

WIN_X = 32
WIN_Y = 32
QX = 128
QY = 128
QZ = 64
LANES = 128
SCALE = 128.0
SMALL = jnp.float8_e4m3fn

LATTICE = 2.8665
POISSON = 0.29
MIX = 1.0 - 2.0 * POISSON
BURGERS_TABLE = np.array(
    [[1.0, 1.0, 1.0], [-1.0, 1.0, 1.0], [1.0, -1.0, 1.0], [1.0, 1.0, -1.0]]
) * (0.5 * LATTICE)
NORMAL_TABLE = (
    np.array(
        [
            [1.0, 1.0, 0.0],
            [1.0, -1.0, 0.0],
            [1.0, 0.0, 1.0],
            [1.0, 0.0, -1.0],
            [0.0, 1.0, 1.0],
            [0.0, 1.0, -1.0],
        ]
    )
    * 0.70710678
)


def fit(function, degree):
    nodes = 0.125 * (1.0 + np.cos(np.pi * (np.arange(64) + 0.5) / 64))
    series = np.polynomial.Chebyshev.fit(nodes, function(np.sqrt(nodes)), degree, domain=[0.0, 0.25])
    return [float(c) for c in series.convert(kind=np.polynomial.Polynomial).coef]


COSINE = fit(lambda r: np.cos(2.0 * np.pi * r), 5)
SINE = fit(lambda r: np.sin(2.0 * np.pi * r) / r, 5)


def horner(coefs, u):
    total = jnp.float32(coefs[-1])
    for c in reversed(coefs[:-1]):
        total = total * u + jnp.float32(c)
    return total


def cos_turns(t):
    r = t - jnp.round(t)
    return horner(COSINE, r * r)


def cos_sin_turns(t):
    r = t - jnp.round(t)
    u = r * r
    return horner(COSINE, u), r * horner(SINE, u)


def lookup(index, table, column):
    total = jnp.zeros(index.shape, jnp.float32)
    for entry in range(table.shape[0]):
        total = jnp.where(index == entry, jnp.float32(table[entry, column]), total)
    return total


def field_phase(
    nl, site_ref, cells_ref, burgers_ref, habit_ref, radius_ref, part_ref, params_ref, anchor_ref
):
    loops = cells_ref.shape[1]
    chunks = site_ref.shape[0]
    rows_each = part_ref.shape[2]
    burgers = [lookup(burgers_ref[...], BURGERS_TABLE, c) for c in range(3)]
    normal = [lookup(habit_ref[...], NORMAL_TABLE, c) for c in range(3)]
    centre = [LATTICE * (cells_ref[c : c + 1, :].astype(jnp.float32) + 0.25) for c in range(3)]
    radius_sq = radius_ref[...] * radius_ref[...]
    overlap = burgers[0] * normal[0] + burgers[1] * normal[1] + burgers[2] * normal[2]
    ratio = 3.0 / MIX
    rows = (
        centre
        + [radius_sq]
        + burgers
        + [ratio * n for n in normal]
        + [(1.0 / ratio) * b for b in burgers]
        + normal
        + [(MIX / (8.0 * (1.0 - POISSON))) * radius_sq, (1.0 / MIX) * overlap]
    )
    count = len(rows)
    rows = rows + [jnp.zeros((1, loops), jnp.float32)] * (-count % 8)
    columns = jnp.concatenate(rows, axis=0).T
    for number in range(count):
        params_ref[number] = jnp.broadcast_to(columns[:, number : number + 1], (loops, LANES))

    site = site_ref[...]
    basis = 0.5 * (site & 1).astype(jnp.float32)
    cell = lax.shift_right_logical(site, 1)
    first = lax.rem(cell, WIN_X)
    second = lax.rem(lax.div(cell, WIN_X), WIN_Y)
    third = lax.div(cell, WIN_X * WIN_Y)
    for axis, index in enumerate((first, second, third)):
        anchor_ref[axis] = LATTICE * (index.astype(jnp.float32) + basis)

    width = 4

    def chunk_step(step, _):
        anchors = [
            [
                jnp.broadcast_to(anchor_ref[axis, pl.ds(step * width + w, 1), :], (8, LANES))
                for axis in range(3)
            ]
            for w in range(width)
        ]

        def loop_step(group, sums):
            at = pl.ds(pl.multiple_of(group * 8, 8), 8)
            p = [params_ref[number, at, :] for number in range(count)]
            new = []
            for w in range(width):
                d = [anchors[w][c] - p[c] for c in range(3)]
                s = d[0] * d[0] + d[1] * d[1] + d[2] * d[2] + p[3]
                root = lax.rsqrt(s)
                inv = root * root
                scale = inv * root * p[16]
                along_b = p[4] * d[0] + p[5] * d[1] + p[6] * d[2]
                along_n = p[7] * d[0] + p[8] * d[1] + p[9] * d[2]
                weight_b = scale * along_n
                weight_n = scale * along_b
                weight_d = scale * (along_b * along_n * inv - p[17])
                for c in range(3):
                    new.append(
                        sums[3 * w + c] + (p[10 + c] * weight_b + p[13 + c] * weight_n + d[c] * weight_d)
                    )
            return tuple(new)

        zero = jnp.zeros((8, LANES), jnp.float32)
        sums = lax.fori_loop(0, loops // 8, loop_step, (zero,) * (3 * width), unroll=2)
        for w in range(width):
            chunk = step * width + w
            for c in range(3):
                total = jnp.sum(sums[3 * w + c], axis=0, keepdims=True)
                part_ref[lax.div(chunk, rows_each), c, pl.ds(lax.rem(chunk, rows_each), 1), :] = (
                    total + (1.0 / nl) * anchor_ref[c, pl.ds(chunk, 1), :]
                )
        return 0

    lax.fori_loop(0, chunks // width, chunk_step, 0)


def split(value):
    high = value.astype(jnp.bfloat16)
    low = value - high.astype(jnp.float32)
    return high, value.astype(SMALL), low.astype(SMALL)


def whole_kernel(
    na, nl, atom_total,
    site_ref, cells_ref, burgers_ref, habit_ref, radius_ref, out_ref,
    params_ref, anchor_ref, part_ref, landed_ref, pos_ref, acc_ref,
    tabs0, tabs1, own_ref, give_ref, take_ref,
    send_a, recv_a, send_b, recv_b, send_c, recv_c, send_d, recv_d,
):
    me_a = lax.axis_index("atoms")
    me_l = lax.axis_index("loops")
    mesh_ids = pl.DeviceIdType.MESH
    chips = na // 2
    core = lax.rem(me_a, 2)
    peers_a = [lax.rem(me_a + 2 * o, na) for o in range(1, chips)]
    peers_l = [lax.rem(me_l + o, nl) for o in range(1, nl)]
    partner = me_a + 1 - 2 * core
    barrier = pltpu.get_barrier_semaphore()
    for peer in peers_a + [partner]:
        pl.semaphore_signal(barrier, inc=1, device_id=(peer, me_l), device_id_type=mesh_ids)
    for peer in peers_l:
        pl.semaphore_signal(barrier, inc=1, device_id=(me_a, peer), device_id_type=mesh_ids)

    field_phase(
        nl, site_ref, cells_ref, burgers_ref, habit_ref, radius_ref, part_ref, params_ref, anchor_ref
    )
    pl.semaphore_wait(barrier, chips + nl - 1)

    def send(src, dst, send_sem, recv_sem, peer):
        copy = pltpu.make_async_remote_copy(
            src_ref=src,
            dst_ref=dst,
            send_sem=send_sem,
            recv_sem=recv_sem,
            device_id=peer,
            device_id_type=mesh_ids,
        )
        copy.start()
        return copy

    first = [
        send(part_ref.at[peer], landed_ref.at[o], send_a.at[o], recv_a.at[o], (me_a, peer))
        for o, peer in enumerate(peers_l)
    ]

    zrows, xhalf, _ = out_ref.shape
    zhalf, yhalf = zrows // 2, QY // 2
    rows = pos_ref.shape[3]
    half = rows // 2
    inverse = 1.0 / LATTICE
    unit = inverse / QX
    pair = lax.div(me_a, 2)
    xmid = 1.0 + (pair * (2 * xhalf) + xhalf - QX // 2).astype(jnp.float32) / QX
    zmid = (me_l * zrows + zhalf - QZ // 2).astype(jnp.float32) / QX

    def sub_iota(count):
        return lax.broadcasted_iota(jnp.int32, (count, LANES), 0)

    znumber = sub_iota(2 * zhalf)
    zsine = znumber >= zhalf
    zfactor = (jnp.where(zsine, znumber - zhalf, znumber).astype(jnp.float32) + 0.5) * unit
    zshift = jnp.where(zsine, 0.25, 0.0).astype(jnp.float32)
    xfactor = (sub_iota(xhalf).astype(jnp.float32) + 0.5) * unit
    fine = (sub_iota(8).astype(jnp.float32) - 3.5) * unit
    blocks = yhalf // 16
    coarse_number = sub_iota(8)
    coarse = jnp.where(
        coarse_number < blocks, 4.0 + 8.0 * coarse_number.astype(jnp.float32), 0.5 * yhalf
    ) * unit

    def tables(x, y, z):
        if zhalf % 8 == 0:
            ztab = jnp.concatenate(cos_sin_turns(z * zfactor[:zhalf]), axis=0)
        else:
            ztab = cos_turns(z * zfactor - zshift)
        ztab = SCALE * ztab
        xtab = cos_sin_turns(x * xfactor)
        base = (x * xmid + z * zmid + y) * inverse
        base = base - jnp.round(base)
        dr, di = cos_sin_turns(base + y * fine)
        dr, di = SCALE * dr, SCALE * di
        cc, cs = cos_sin_turns(y * coarse)
        left = jnp.concatenate(
            [xtab[t][n : n + 1, :] * ztab for t in range(2) for n in range(xhalf)], axis=0
        )
        real = [None] * (2 * blocks)
        imag = [None] * (2 * blocks)
        for k in range(blocks):
            c, s = cc[k : k + 1, :], cs[k : k + 1, :]
            rc, rs, ic, is_ = dr * c, dr * s, di * c, di * s
            real[blocks + k], imag[blocks + k] = rc - is_, ic + rs
            real[blocks - 1 - k], imag[blocks - 1 - k] = rc + is_, ic - rs
        turned = jnp.concatenate(real + imag, axis=0)
        right = jnp.concatenate(
            [turned * cc[blocks : blocks + 1, :], turned * cs[blocks : blocks + 1, :]], axis=0
        )
        return split(left), split(right)

    def build(quarter, slot, begin, span, tabs):
        for r in range(*span):
            x, y, z = (pos_ref[quarter, slot, c, begin + r : begin + r + 1, :] for c in range(3))
            left, right = tables(x, y, z)
            lanes = slice(r * LANES, (r + 1) * LANES)
            for n, value in enumerate(left + right):
                tabs[n][:, lanes] = value

    def dot(a, b):
        return lax.dot_general(
            a, b, (((1,), (1,)), ((), ())), preferred_element_type=jnp.float32
        )

    def multiply_high(tabs):
        acc_ref[...] += dot(tabs[0][...], tabs[3][...])

    def multiply_rest(tabs):
        lq, ll, rq, rl = (tabs[n][...] for n in (1, 2, 4, 5))
        acc_ref[...] += dot(jnp.concatenate([ll, lq], axis=1), jnp.concatenate([rq, rl], axis=1))

    middle = half // 2

    def process(quarter, begin, end):
        def step(slot, _):
            for begin, tabs, ready in ((0, tabs0, tabs1), (half, tabs1, tabs0)):
                multiply_high(ready)
                build(quarter, slot, begin, (0, middle), tabs)
                multiply_rest(ready)
                build(quarter, slot, begin, (middle, half), tabs)
            return 0

        lax.fori_loop(begin, end, step, 0)

    acc_ref[...] = jnp.zeros_like(acc_ref)
    for ref in tabs1:
        ref[...] = jnp.zeros_like(ref)
    total = part_ref[me_l]
    for o, copy in enumerate(first):
        copy.wait_recv()
        total = total + landed_ref[o]
    pos_ref[0, 0] = total
    second = [
        send(pos_ref.at[0, 0], pos_ref.at[0, o + 1], send_b.at[o], recv_b.at[o], (peer, me_l))
        for o, peer in enumerate(peers_a)
    ]
    process(0, 0, 1)
    for copy in second:
        copy.wait_recv()
    third = [
        send(pos_ref.at[0], pos_ref.at[o + 1], send_c.at[o], recv_c.at[o], (me_a, peer))
        for o, peer in enumerate(peers_l)
    ]
    process(0, 1, chips)
    for o, copy in enumerate(third):
        copy.wait_recv()
        process(o + 1, 0, chips)
    multiply_high(tabs1)
    multiply_rest(tabs1)

    mine = (2 * core - 1).astype(jnp.float32)
    width = 2 * zhalf

    def combine(begin):
        block = acc_ref[begin : begin + width, :]
        cre, cim = block[:, :yhalf], block[:, yhalf : 2 * yhalf]
        sre, sim = block[:, 2 * yhalf : 3 * yhalf], block[:, 3 * yhalf :]
        re = jnp.concatenate([cre + sim, cre - sim], axis=1)
        im = jnp.concatenate([cim - sre, cim + sre], axis=1)
        rc, rs, ic, is_ = re[:zhalf], re[zhalf:], im[:zhalf], im[zhalf:]
        return ((rc + is_, ic - rs), (rc - is_, ic + rs))

    pieces = math.gcd(4, xhalf)
    each = xhalf // pieces
    fourth = []
    for piece in range(pieces):
        for mx in range(piece * each, (piece + 1) * each):
            of_cos = combine(mx * width)
            of_sin = combine((xhalf + mx) * width)
            for zsign in range(2):
                rc, ic = of_cos[zsign]
                rs, is_ = of_sin[zsign][0] * mine, of_sin[zsign][1] * mine
                own_ref[mx, zsign, 0], own_ref[mx, zsign, 1] = rc - is_, ic + rs
                give_ref[mx, zsign, 0], give_ref[mx, zsign, 1] = rc + is_, ic - rs
        at = pl.ds(piece * each, each)
        fourth.append(
            send(give_ref.at[at], take_ref.at[at], send_d.at[piece], recv_d.at[piece], (partner, me_l))
        )
    for piece in range(pieces):
        fourth[piece].wait_recv()
        for mx in range(piece * each, (piece + 1) * each):
            place = core * mx + (1 - core) * (xhalf - 1 - mx)
            for zsign in range(2):
                re = own_ref[mx, zsign, 0] + take_ref[mx, zsign, 0]
                im = own_ref[mx, zsign, 1] + take_ref[mx, zsign, 1]
                value = jnp.log1p((re * re + im * im) / atom_total)
                for mz in range(zhalf):
                    zi = zhalf + mz if zsign else zhalf - 1 - mz
                    out_ref[zi, pl.ds(place, 1), :] = value[mz : mz + 1, :]
    for copy in first + second + third + fourth:
        copy.wait_send()


def body(na, nl, atom_site, loop_cells, loop_burgers, loop_habit, loop_radius):
    atoms = atom_site.shape[0]
    loops = loop_cells.shape[1]
    chunks = atoms // LANES
    rows = chunks // nl
    zrows, xrows = QZ // nl, QX // na
    height = 2 * zrows * xrows
    depth = rows // 2 * LANES
    vmem = pl.BlockSpec(memory_space=pltpu.VMEM)
    f32, bf16 = jnp.float32, jnp.bfloat16
    half_block = (xrows, 2, 2, zrows // 2, QY)
    scratch = [
        pltpu.VMEM((18, loops, LANES), f32),
        pltpu.VMEM((3, chunks, LANES), f32),
        pltpu.VMEM((nl, 3, rows, LANES), f32),
        pltpu.VMEM((nl - 1, 3, rows, LANES), f32),
        pltpu.VMEM((nl, na // 2, 3, rows, LANES), f32),
        pltpu.VMEM((height, 2 * QY), f32),
    ]
    table = tuple(
        pltpu.VMEM((count, depth), kind) for count in (height, 2 * QY) for kind in (bf16, SMALL, SMALL)
    )
    scratch += [table, table]
    scratch += [pltpu.VMEM(half_block, f32)] * 3
    counts = (nl - 1, nl - 1, na // 2 - 1, na // 2 - 1, nl - 1, nl - 1, 4, 4)
    scratch += [pltpu.SemaphoreType.DMA((n,)) for n in counts]
    return pl.pallas_call(
        functools.partial(whole_kernel, na, nl, SCALE**4 * atoms * na),
        out_shape=jax.ShapeDtypeStruct((zrows, xrows, QY), f32),
        in_specs=[vmem] * 5,
        out_specs=vmem,
        scratch_shapes=scratch,
        compiler_params=pltpu.CompilerParams(
            collective_id=0, has_side_effects=True, vmem_limit_bytes=48 * 2**20
        ),
        name="diffuse",
    )(
        atom_site.reshape(chunks, LANES),
        loop_cells,
        loop_burgers.reshape(1, loops),
        loop_habit.reshape(1, loops),
        loop_radius.reshape(1, loops),
    )


def solution(mesh):
    placed = (P("atoms"), P(None, "loops"), P("loops"), P("loops"), P("loops"))
    return jax.shard_map(
        functools.partial(body, mesh.shape["atoms"], mesh.shape["loops"]),
        mesh=mesh,
        in_specs=placed,
        out_specs=P("loops", "atoms", None),
        check_vma=False,
    )
```

```python
import functools
import math

import jax
import jax.numpy as jnp
import numpy as np
from jax import lax
from jax.experimental import pallas as pl
from jax.experimental.pallas import tpu as pltpu
from jax.sharding import PartitionSpec as P

WIN_X = 32
WIN_Y = 32
QX = 128
QY = 128
QZ = 64
LANES = 128
SCALE = 128.0
SMALL = jnp.float8_e4m3fn

LATTICE = 2.8665
POISSON = 0.29
MIX = 1.0 - 2.0 * POISSON
BURGERS_TABLE = np.array(
    [[1.0, 1.0, 1.0], [-1.0, 1.0, 1.0], [1.0, -1.0, 1.0], [1.0, 1.0, -1.0]]
) * (0.5 * LATTICE)
NORMAL_TABLE = (
    np.array(
        [
            [1.0, 1.0, 0.0],
            [1.0, -1.0, 0.0],
            [1.0, 0.0, 1.0],
            [1.0, 0.0, -1.0],
            [0.0, 1.0, 1.0],
            [0.0, 1.0, -1.0],
        ]
    )
    * 0.70710678
)


def fit(function, degree):
    nodes = 0.125 * (1.0 + np.cos(np.pi * (np.arange(64) + 0.5) / 64))
    series = np.polynomial.Chebyshev.fit(nodes, function(np.sqrt(nodes)), degree, domain=[0.0, 0.25])
    return [float(c) for c in series.convert(kind=np.polynomial.Polynomial).coef]


COSINE = fit(lambda r: np.cos(2.0 * np.pi * r), 5)
SINE = fit(lambda r: np.sin(2.0 * np.pi * r) / r, 5)


def horner(coefs, u):
    total = jnp.float32(coefs[-1])
    for c in reversed(coefs[:-1]):
        total = total * u + jnp.float32(c)
    return total


def cos_turns(t):
    r = t - jnp.round(t)
    return horner(COSINE, r * r)


def cos_sin_turns(t):
    r = t - jnp.round(t)
    u = r * r
    return horner(COSINE, u), r * horner(SINE, u)


def lookup(index, table, column):
    total = jnp.zeros(index.shape, jnp.float32)
    for entry in range(table.shape[0]):
        total = jnp.where(index == entry, jnp.float32(table[entry, column]), total)
    return total


def field_phase(
    nl, site_ref, cells_ref, burgers_ref, habit_ref, radius_ref, part_ref, params_ref, anchor_ref
):
    loops = cells_ref.shape[1]
    chunks = site_ref.shape[0]
    rows_each = part_ref.shape[2]
    burgers = [lookup(burgers_ref[...], BURGERS_TABLE, c) for c in range(3)]
    normal = [lookup(habit_ref[...], NORMAL_TABLE, c) for c in range(3)]
    centre = [LATTICE * (cells_ref[c : c + 1, :].astype(jnp.float32) + 0.25) for c in range(3)]
    radius_sq = radius_ref[...] * radius_ref[...]
    overlap = burgers[0] * normal[0] + burgers[1] * normal[1] + burgers[2] * normal[2]
    ratio = 3.0 / MIX
    rows = (
        centre
        + [radius_sq]
        + burgers
        + [ratio * n for n in normal]
        + [(1.0 / ratio) * b for b in burgers]
        + normal
        + [(MIX / (8.0 * (1.0 - POISSON))) * radius_sq, (1.0 / MIX) * overlap]
    )
    count = len(rows)
    rows = rows + [jnp.zeros((1, loops), jnp.float32)] * (-count % 8)
    columns = jnp.concatenate(rows, axis=0).T
    for number in range(count):
        params_ref[number] = jnp.broadcast_to(columns[:, number : number + 1], (loops, LANES))

    site = site_ref[...]
    basis = 0.5 * (site & 1).astype(jnp.float32)
    cell = lax.shift_right_logical(site, 1)
    first = lax.rem(cell, WIN_X)
    second = lax.rem(lax.div(cell, WIN_X), WIN_Y)
    third = lax.div(cell, WIN_X * WIN_Y)
    for axis, index in enumerate((first, second, third)):
        anchor_ref[axis] = LATTICE * (index.astype(jnp.float32) + basis)

    width = 4

    def chunk_step(step, _):
        anchors = [
            [
                jnp.broadcast_to(anchor_ref[axis, pl.ds(step * width + w, 1), :], (8, LANES))
                for axis in range(3)
            ]
            for w in range(width)
        ]

        def loop_step(group, sums):
            at = pl.ds(pl.multiple_of(group * 8, 8), 8)
            p = [params_ref[number, at, :] for number in range(count)]
            new = []
            for w in range(width):
                d = [anchors[w][c] - p[c] for c in range(3)]
                s = d[0] * d[0] + d[1] * d[1] + d[2] * d[2] + p[3]
                root = lax.rsqrt(s)
                inv = root * root
                scale = inv * root * p[16]
                along_b = p[4] * d[0] + p[5] * d[1] + p[6] * d[2]
                along_n = p[7] * d[0] + p[8] * d[1] + p[9] * d[2]
                weight_b = scale * along_n
                weight_n = scale * along_b
                weight_d = scale * (along_b * along_n * inv - p[17])
                for c in range(3):
                    new.append(
                        sums[3 * w + c] + (p[10 + c] * weight_b + p[13 + c] * weight_n + d[c] * weight_d)
                    )
            return tuple(new)

        zero = jnp.zeros((8, LANES), jnp.float32)
        sums = lax.fori_loop(0, loops // 8, loop_step, (zero,) * (3 * width), unroll=4)
        for w in range(width):
            chunk = step * width + w
            for c in range(3):
                total = jnp.sum(sums[3 * w + c], axis=0, keepdims=True)
                part_ref[lax.div(chunk, rows_each), c, pl.ds(lax.rem(chunk, rows_each), 1), :] = (
                    total + (1.0 / nl) * anchor_ref[c, pl.ds(chunk, 1), :]
                )
        return 0

    lax.fori_loop(0, chunks // width, chunk_step, 0)


def split(value):
    high = value.astype(jnp.bfloat16)
    low = value - high.astype(jnp.float32)
    return high, value.astype(SMALL), low.astype(SMALL)


def whole_kernel(
    na, nl, atom_total,
    site_any, cells_any, burgers_any, habit_any, radius_any, out_ref,
    site_ref, cells_ref, burgers_ref, habit_ref, radius_ref, fetched,
    params_ref, anchor_ref, part_ref, landed_ref, pos_ref, acc_ref,
    tabs0, tabs1, own_ref, give_ref, take_ref,
    send_a, recv_a, send_b, recv_b, send_c, recv_c, send_d, recv_d,
):
    fetches = [
        pltpu.make_async_copy(source, held, fetched.at[n])
        for n, (source, held) in enumerate(
            (
                (site_any, site_ref),
                (cells_any, cells_ref),
                (burgers_any, burgers_ref),
                (habit_any, habit_ref),
                (radius_any, radius_ref),
            )
        )
    ]
    for copy in fetches:
        copy.start()
    me_a = lax.axis_index("atoms")
    me_l = lax.axis_index("loops")
    mesh_ids = pl.DeviceIdType.MESH
    chips = na // 2
    core = lax.rem(me_a, 2)
    peers_a = [lax.rem(me_a + 2 * o, na) for o in range(1, chips)]
    peers_l = [lax.rem(me_l + o, nl) for o in range(1, nl)]
    partner = me_a + 1 - 2 * core
    barrier = pltpu.get_barrier_semaphore()
    for peer in peers_a + [partner]:
        pl.semaphore_signal(barrier, inc=1, device_id=(peer, me_l), device_id_type=mesh_ids)
    for peer in peers_l:
        pl.semaphore_signal(barrier, inc=1, device_id=(me_a, peer), device_id_type=mesh_ids)

    for copy in fetches:
        copy.wait()
    field_phase(
        nl, site_ref, cells_ref, burgers_ref, habit_ref, radius_ref, part_ref, params_ref, anchor_ref
    )
    pl.semaphore_wait(barrier, chips + nl - 1)

    def send(src, dst, send_sem, recv_sem, peer):
        copy = pltpu.make_async_remote_copy(
            src_ref=src,
            dst_ref=dst,
            send_sem=send_sem,
            recv_sem=recv_sem,
            device_id=peer,
            device_id_type=mesh_ids,
        )
        copy.start()
        return copy

    first = [
        send(part_ref.at[peer], landed_ref.at[o], send_a.at[o], recv_a.at[o], (me_a, peer))
        for o, peer in enumerate(peers_l)
    ]

    zrows, xhalf, _ = out_ref.shape
    zhalf, yhalf = zrows // 2, QY // 2
    rows = pos_ref.shape[3]
    half = rows // 2
    inverse = 1.0 / LATTICE
    unit = inverse / QX
    pair = lax.div(me_a, 2)
    xmid = 1.0 + (pair * (2 * xhalf) + xhalf - QX // 2).astype(jnp.float32) / QX
    zmid = (me_l * zrows + zhalf - QZ // 2).astype(jnp.float32) / QX

    def sub_iota(count):
        return lax.broadcasted_iota(jnp.int32, (count, LANES), 0)

    znumber = sub_iota(2 * zhalf)
    zsine = znumber >= zhalf
    zfactor = (jnp.where(zsine, znumber - zhalf, znumber).astype(jnp.float32) + 0.5) * unit
    zshift = jnp.where(zsine, 0.25, 0.0).astype(jnp.float32)
    xfactor = (sub_iota(xhalf).astype(jnp.float32) + 0.5) * unit
    fine = (sub_iota(8).astype(jnp.float32) - 3.5) * unit
    blocks = yhalf // 16
    coarse_number = sub_iota(8)
    coarse = jnp.where(
        coarse_number < blocks, 4.0 + 8.0 * coarse_number.astype(jnp.float32), 0.5 * yhalf
    ) * unit

    def tables(x, y, z):
        if zhalf % 8 == 0:
            ztab = jnp.concatenate(cos_sin_turns(z * zfactor[:zhalf]), axis=0)
        else:
            ztab = cos_turns(z * zfactor - zshift)
        ztab = SCALE * ztab
        xtab = cos_sin_turns(x * xfactor)
        base = (x * xmid + z * zmid + y) * inverse
        base = base - jnp.round(base)
        dr, di = cos_sin_turns(base + y * fine)
        dr, di = SCALE * dr, SCALE * di
        cc, cs = cos_sin_turns(y * coarse)
        left = jnp.concatenate(
            [xtab[t][n : n + 1, :] * ztab for t in range(2) for n in range(xhalf)], axis=0
        )
        real = [None] * (2 * blocks)
        imag = [None] * (2 * blocks)
        for k in range(blocks):
            c, s = cc[k : k + 1, :], cs[k : k + 1, :]
            rc, rs, ic, is_ = dr * c, dr * s, di * c, di * s
            real[blocks + k], imag[blocks + k] = rc - is_, ic + rs
            real[blocks - 1 - k], imag[blocks - 1 - k] = rc + is_, ic - rs
        turned = jnp.concatenate(real + imag, axis=0)
        right = jnp.concatenate(
            [turned * cc[blocks : blocks + 1, :], turned * cs[blocks : blocks + 1, :]], axis=0
        )
        return split(left), split(right)

    def build(quarter, slot, begin, span, tabs):
        for r in range(*span):
            x, y, z = (pos_ref[quarter, slot, c, begin + r : begin + r + 1, :] for c in range(3))
            left, right = tables(x, y, z)
            lanes = slice(r * LANES, (r + 1) * LANES)
            for n, value in enumerate(left + right):
                tabs[n][:, lanes] = value

    def dot(a, b):
        return lax.dot_general(
            a, b, (((1,), (1,)), ((), ())), preferred_element_type=jnp.float32
        )

    def multiply_high(tabs):
        acc_ref[...] += dot(tabs[0][...], tabs[3][...])

    def multiply_rest(tabs):
        lq, ll, rq, rl = (tabs[n][...] for n in (1, 2, 4, 5))
        acc_ref[...] += dot(jnp.concatenate([ll, lq], axis=1), jnp.concatenate([rq, rl], axis=1))

    middle = half // 2

    def process(quarter, begin, end):
        def step(slot, _):
            for begin, tabs, ready in ((0, tabs0, tabs1), (half, tabs1, tabs0)):
                multiply_high(ready)
                build(quarter, slot, begin, (0, middle), tabs)
                multiply_rest(ready)
                build(quarter, slot, begin, (middle, half), tabs)
            return 0

        lax.fori_loop(begin, end, step, 0)

    acc_ref[...] = jnp.zeros_like(acc_ref)
    for ref in tabs1:
        ref[...] = jnp.zeros_like(ref)
    total = part_ref[me_l]
    for o, copy in enumerate(first):
        copy.wait_recv()
        total = total + landed_ref[o]
    pos_ref[0, 0] = total
    second = [
        send(pos_ref.at[0, 0], pos_ref.at[0, o + 1], send_b.at[o], recv_b.at[o], (peer, me_l))
        for o, peer in enumerate(peers_a)
    ]
    process(0, 0, 1)
    for copy in second:
        copy.wait_recv()
    third = [
        send(pos_ref.at[0], pos_ref.at[o + 1], send_c.at[o], recv_c.at[o], (me_a, peer))
        for o, peer in enumerate(peers_l)
    ]
    process(0, 1, chips)
    for o, copy in enumerate(third):
        copy.wait_recv()
        process(o + 1, 0, chips)
    multiply_high(tabs1)
    multiply_rest(tabs1)

    mine = (2 * core - 1).astype(jnp.float32)
    width = 2 * zhalf

    def combine(begin):
        block = acc_ref[begin : begin + width, :]
        cre, cim = block[:, :yhalf], block[:, yhalf : 2 * yhalf]
        sre, sim = block[:, 2 * yhalf : 3 * yhalf], block[:, 3 * yhalf :]
        re = jnp.concatenate([cre + sim, cre - sim], axis=1)
        im = jnp.concatenate([cim - sre, cim + sre], axis=1)
        rc, rs, ic, is_ = re[:zhalf], re[zhalf:], im[:zhalf], im[zhalf:]
        return ((rc + is_, ic - rs), (rc - is_, ic + rs))

    pieces = math.gcd(4, xhalf)
    each = xhalf // pieces
    fourth = []
    for piece in range(pieces):
        for mx in range(piece * each, (piece + 1) * each):
            of_cos = combine(mx * width)
            of_sin = combine((xhalf + mx) * width)
            for zsign in range(2):
                rc, ic = of_cos[zsign]
                rs, is_ = of_sin[zsign][0] * mine, of_sin[zsign][1] * mine
                own_ref[mx, zsign, 0], own_ref[mx, zsign, 1] = rc - is_, ic + rs
                give_ref[mx, zsign, 0], give_ref[mx, zsign, 1] = rc + is_, ic - rs
        at = pl.ds(piece * each, each)
        fourth.append(
            send(give_ref.at[at], take_ref.at[at], send_d.at[piece], recv_d.at[piece], (partner, me_l))
        )
    for piece in range(pieces):
        fourth[piece].wait_recv()
        for mx in range(piece * each, (piece + 1) * each):
            place = core * mx + (1 - core) * (xhalf - 1 - mx)
            for zsign in range(2):
                re = own_ref[mx, zsign, 0] + take_ref[mx, zsign, 0]
                im = own_ref[mx, zsign, 1] + take_ref[mx, zsign, 1]
                value = jnp.log1p((re * re + im * im) / atom_total)
                for mz in range(zhalf):
                    zi = zhalf + mz if zsign else zhalf - 1 - mz
                    out_ref[zi, pl.ds(place, 1), :] = value[mz : mz + 1, :]
    for copy in first + second + third + fourth:
        copy.wait_send()


def body(na, nl, atom_site, loop_cells, loop_burgers, loop_habit, loop_radius):
    atoms = atom_site.shape[0]
    loops = loop_cells.shape[1]
    chunks = atoms // LANES
    rows = chunks // nl
    zrows, xrows = QZ // nl, QX // na
    height = 2 * zrows * xrows
    depth = rows // 2 * LANES
    vmem = pl.BlockSpec(memory_space=pltpu.VMEM)
    f32, bf16 = jnp.float32, jnp.bfloat16
    half_block = (xrows, 2, 2, zrows // 2, QY)
    scratch = [
        pltpu.VMEM((chunks, LANES), jnp.int32),
        pltpu.VMEM((3, loops), jnp.int32),
        pltpu.VMEM((1, loops), jnp.int32),
        pltpu.VMEM((1, loops), jnp.int32),
        pltpu.VMEM((1, loops), f32),
        pltpu.SemaphoreType.DMA((5,)),
        pltpu.VMEM((18, loops, LANES), f32),
        pltpu.VMEM((3, chunks, LANES), f32),
        pltpu.VMEM((nl, 3, rows, LANES), f32),
        pltpu.VMEM((nl - 1, 3, rows, LANES), f32),
        pltpu.VMEM((nl, na // 2, 3, rows, LANES), f32),
        pltpu.VMEM((height, 2 * QY), f32),
    ]
    table = tuple(
        pltpu.VMEM((count, depth), kind) for count in (height, 2 * QY) for kind in (bf16, SMALL, SMALL)
    )
    scratch += [table, table]
    scratch += [pltpu.VMEM(half_block, f32)] * 3
    counts = (nl - 1, nl - 1, na // 2 - 1, na // 2 - 1, nl - 1, nl - 1, 4, 4)
    scratch += [pltpu.SemaphoreType.DMA((n,)) for n in counts]
    return pl.pallas_call(
        functools.partial(whole_kernel, na, nl, SCALE**4 * atoms * na),
        out_shape=jax.ShapeDtypeStruct((zrows, xrows, QY), f32),
        in_specs=[pl.BlockSpec(memory_space=pl.ANY)] * 5,
        out_specs=vmem,
        scratch_shapes=scratch,
        compiler_params=pltpu.CompilerParams(
            collective_id=0, has_side_effects=True, vmem_limit_bytes=48 * 2**20
        ),
        name="diffuse",
    )(
        atom_site.reshape(chunks, LANES),
        loop_cells,
        loop_burgers.reshape(1, loops),
        loop_habit.reshape(1, loops),
        loop_radius.reshape(1, loops),
    )


def solution(mesh):
    placed = (P("atoms"), P(None, "loops"), P("loops"), P("loops"), P("loops"))
    return jax.shard_map(
        functools.partial(body, mesh.shape["atoms"], mesh.shape["loops"]),
        mesh=mesh,
        in_specs=placed,
        out_specs=P("loops", "atoms", None),
        check_vma=False,
    )
```
